512 devices in a mesh: dp: 2 (over x_lo), ctx: 32 (over x_hi, z), head: 8 (over y, core).
Axes of the slice: x: 4 (x_hi: 2, x_lo: 2; x = x_hi * 2 + x_lo), y: 4, z: 16, core: 2. Of those that a mesh axis runs over, the one named last changes fastest.
Arguments:
- queries: bfloat16 [2, 32768, 4096], P('dp', ('ctx', 'head')), may hold values from -6 to 6
- keys: bfloat16 [2, 32768, 1024], P('dp', ('ctx', 'head')), may hold values from -6 to 6
- values: bfloat16 [2, 32768, 1024], P('dp', ('ctx', 'head')), may hold values from -6 to 6
- output_gradient_stored: bfloat16 [2, 32768, 4096], P('dp', ('ctx', 'head')), may hold values from -41 to 41
Outputs:
- grad_queries: bfloat16 [2, 32768, 4096], P('dp', ('ctx', 'head'))
- key_gradient_rows: bfloat16 [2, 32768, 1024], P('dp', ('ctx', 'head'))
- value_gradient_rows: bfloat16 [2, 32768, 1024], P('dp', ('ctx', 'head'))
- grad_norm: float32 [], replicated
The draws below stay inside these ranges and needn't reach their ends.
All inputs are finite; a program needn't handle non-finite values.
Results may differ from the reference program's by a relative error of at most 0.02.
Values may be sent and summed in bfloat16 or wider, within the bound.
No kernel may reach another device: no remote copies, remote signals or barrier semaphores. Data moves between devices by JAX's collectives and lax.ppermute only.
A program may use at most 64 MiB of HBM per device.

```python
import jax
import jax.numpy as jnp
from jax import lax

BLOCK_POSITIONS = 512
HEAD_SIZE = 128
QUERY_HEADS = 32
KEY_VALUE_HEADS = 8
SEQUENCE_COUNT = 2
SEQUENCE_LENGTH = 32768


def draw_queries(key, part):
    key = jax.random.fold_in(key, 1)
    query_group_width = QUERY_HEADS // KEY_VALUE_HEADS
    base_offset = jnp.clip(jax.random.normal(key, (SEQUENCE_COUNT, SEQUENCE_LENGTH, KEY_VALUE_HEADS, query_group_width, HEAD_SIZE), jnp.float32), -6.0, 6.0)
    return base_offset.reshape(SEQUENCE_COUNT, SEQUENCE_LENGTH, QUERY_HEADS * HEAD_SIZE).astype(jnp.bfloat16)


def draw_keys(key, part):
    key = jax.random.fold_in(key, 2)
    base_offset = jnp.clip(jax.random.normal(key, (SEQUENCE_COUNT, SEQUENCE_LENGTH, KEY_VALUE_HEADS, HEAD_SIZE), jnp.float32), -6.0, 6.0)
    return base_offset.reshape(SEQUENCE_COUNT, SEQUENCE_LENGTH, KEY_VALUE_HEADS * HEAD_SIZE).astype(jnp.bfloat16)


def draw_output_gradient_stored(key, part):
    key = jax.random.fold_in(key, 3)
    rows = jnp.arange(SEQUENCE_LENGTH)
    block_count = SEQUENCE_LENGTH // BLOCK_POSITIONS
    stored_block = rows // BLOCK_POSITIONS
    actual_block = jnp.where(stored_block % 2 == 0, stored_block // 2, block_count - 1 - stored_block // 2)
    position = (actual_block * BLOCK_POSITIONS + rows % BLOCK_POSITIONS).astype(jnp.float32) / SEQUENCE_LENGTH
    head_share = jnp.arange(QUERY_HEADS).astype(jnp.float32) / QUERY_HEADS
    seq_share = jnp.arange(SEQUENCE_COUNT).astype(jnp.float32) / max(SEQUENCE_COUNT - 1, 1)
    scales = 0.25 * jnp.power(3.0, position[None, :, None] + head_share[None, None, :] + seq_share[:, None, None])
    base_offset = jnp.clip(jax.random.normal(key, (SEQUENCE_COUNT, SEQUENCE_LENGTH, QUERY_HEADS, HEAD_SIZE), jnp.float32), -6.0, 6.0)
    return (base_offset * scales[..., None]).reshape(SEQUENCE_COUNT, SEQUENCE_LENGTH, QUERY_HEADS * HEAD_SIZE).astype(jnp.bfloat16)


def steps_of(rng, shape, pieces, least, high):
    def one(dim, shards_of):
        draws = jax.random.uniform(jax.random.fold_in(jax.random.fold_in(rng, 6), dim), (shards_of,), jnp.float32, least / len(pieces), high / len(pieces))
        return jnp.repeat(jnp.exp(draws), shape[dim] // shards_of).reshape((-1,) + (1,) * (len(shape) - dim - 1))

    factor_of = one(*pieces[0])
    for cut in pieces[1:]:
        factor_of = factor_of * one(*cut)
    return factor_of


def bell_draw(stream_key, shape, deviation, limit, split=(), kind=jnp.bfloat16):
    array = deviation * jax.random.normal(stream_key, shape, jnp.float32)
    if split:
        array = array * steps_of(stream_key, shape, split, -0.22, 0.18)
    return jnp.clip(array, -limit, limit).astype(kind)


def setup_inputs(seed: int = 0) -> dict:
    streams_of = jax.random.split(jax.random.key(seed), 5)
    return {
        "queries": draw_queries(jax.random.fold_in(streams_of[4], 71), 0),
        "keys": draw_keys(jax.random.fold_in(streams_of[4], 71), 0),
        "values": bell_draw(streams_of[2], (SEQUENCE_COUNT, SEQUENCE_LENGTH, KEY_VALUE_HEADS * HEAD_SIZE), 1.0, 6.0, ((0, 2), (1, 256))),
        "output_gradient_stored": draw_output_gradient_stored(jax.random.fold_in(streams_of[4], 71), 0),
    }


NEG_FILL = -1e+30

def attend(query_rows, grad_rows, key_own, value_own, key_prev, value_prev, prev_valid):
    scale_factor = query_rows.shape[-1] ** (-0.5)
    positions = jnp.arange(query_rows.shape[0], dtype=jnp.int32)
    own_mask = positions[None, :] <= positions[:, None]
    prev_mask = jnp.broadcast_to(prev_valid, own_mask.shape)
    query_wide = query_rows.astype(jnp.float32)
    grad_wide = grad_rows.astype(jnp.float32)
    key_own_wide = key_own.astype(jnp.float32)
    key_prev_wide = key_prev.astype(jnp.float32)
    value_own_wide = value_own.astype(jnp.float32)
    value_prev_wide = value_prev.astype(jnp.float32)
    score_own = jnp.einsum('igkd,jgd->gkij', query_wide, key_own_wide) * scale_factor
    score_prev = jnp.einsum('igkd,jgd->gkij', query_wide, key_prev_wide) * scale_factor
    score_own = jnp.where(own_mask, score_own, NEG_FILL)
    score_prev = jnp.where(prev_mask, score_prev, NEG_FILL)
    row_top = jnp.maximum(lax.optimization_barrier(jnp.max(score_own, axis=-1)), lax.optimization_barrier(jnp.max(score_prev, axis=-1)))[..., None]
    expo_own = jnp.exp(score_own - row_top)
    expo_prev = jnp.exp(score_prev - row_top)
    row_total = lax.optimization_barrier(jnp.sum(expo_own, axis=-1, keepdims=True)) + lax.optimization_barrier(jnp.sum(expo_prev, axis=-1, keepdims=True))
    prob_own = expo_own / row_total
    prob_prev = expo_prev / row_total
    narrow_own = lax.optimization_barrier(prob_own.astype(jnp.bfloat16)).astype(jnp.float32)
    narrow_prev = lax.optimization_barrier(prob_prev.astype(jnp.bfloat16)).astype(jnp.float32)
    attn_out = jnp.einsum('gkij,jgd->igkd', narrow_own, value_own_wide) + jnp.einsum('gkij,jgd->igkd', narrow_prev, value_prev_wide)
    attn_out = lax.optimization_barrier(attn_out.astype(jnp.bfloat16)).astype(jnp.float32)
    row_delta = jnp.transpose(lax.optimization_barrier(jnp.sum(grad_wide * attn_out, axis=-1)), (1, 2, 0))[..., None]
    dprob_own = jnp.einsum('igkd,jgd->gkij', grad_wide, value_own_wide)
    dprob_prev = jnp.einsum('igkd,jgd->gkij', grad_wide, value_prev_wide)
    dscore_own = lax.optimization_barrier((prob_own * (dprob_own - row_delta) * scale_factor).astype(jnp.bfloat16)).astype(jnp.float32)
    dscore_prev = lax.optimization_barrier((prob_prev * (dprob_prev - row_delta) * scale_factor).astype(jnp.bfloat16)).astype(jnp.float32)
    grad_query = jnp.einsum('gkij,jgd->igkd', dscore_own, key_own_wide) + jnp.einsum('gkij,jgd->igkd', dscore_prev, key_prev_wide)
    grad_key_own = jnp.einsum('gkij,igkd->jgd', dscore_own, query_wide)
    grad_value_own = jnp.einsum('gkij,igkd->jgd', narrow_own, grad_wide)
    grad_key_prev = jnp.einsum('gkij,igkd->jgd', dscore_prev, query_wide)
    grad_value_prev = jnp.einsum('gkij,igkd->jgd', narrow_prev, grad_wide)
    return (grad_query, grad_key_own, grad_value_own, grad_key_prev, grad_value_prev)

def reference(queries, keys, values, output_gradient_stored):
    sequence_total = queries.shape[0]
    sequence_span_length = queries.shape[1]
    number_of_spans = sequence_span_length // BLOCK_POSITIONS
    query_group_width = QUERY_HEADS // KEY_VALUE_HEADS
    actual = jnp.arange(number_of_spans, dtype=jnp.int32)
    stored_position_of = jnp.where(actual < number_of_spans // 2, 2 * actual, 2 * (number_of_spans - 1 - actual) + 1).astype(jnp.int32)
    actual_position_of = jnp.where(actual % 2 == 0, actual // 2, number_of_spans - 1 - actual // 2).astype(jnp.int32)
    query_natural_order = queries.reshape(sequence_total, number_of_spans, BLOCK_POSITIONS, KEY_VALUE_HEADS, query_group_width, HEAD_SIZE)[:, stored_position_of]
    gradient_natural_order = output_gradient_stored.reshape(sequence_total, number_of_spans, BLOCK_POSITIONS, KEY_VALUE_HEADS, query_group_width, HEAD_SIZE)[:, stored_position_of]
    key_natural_order = keys.reshape(sequence_total, number_of_spans, BLOCK_POSITIONS, KEY_VALUE_HEADS, HEAD_SIZE)[:, stored_position_of]
    value_natural_order = values.reshape(sequence_total, number_of_spans, BLOCK_POSITIONS, KEY_VALUE_HEADS, HEAD_SIZE)[:, stored_position_of]

    def one_span(flat_id):
        seq_id = flat_id // number_of_spans
        span_id = flat_id % number_of_spans
        prev_id = jnp.maximum(span_id - 1, 0)
        return attend(query_natural_order[seq_id, span_id], gradient_natural_order[seq_id, span_id], key_natural_order[seq_id, span_id], value_natural_order[seq_id, span_id], key_natural_order[seq_id, prev_id], value_natural_order[seq_id, prev_id], span_id > 0)
    results = lax.map(one_span, jnp.arange(sequence_total * number_of_spans, dtype=jnp.int32))
    shaped = [result_part.reshape((sequence_total, number_of_spans) + result_part.shape[1:]) for result_part in results]
    grad_query, key_own, value_own, key_prev, value_prev = shaped
    zero_span = jnp.zeros_like(key_prev[:, :1])
    grad_key = key_own + jnp.concatenate((key_prev[:, 1:], zero_span), axis=1)
    grad_value = value_own + jnp.concatenate((value_prev[:, 1:], zero_span), axis=1)
    query_low = grad_query.astype(jnp.bfloat16)
    key_reduced_precision = grad_key.astype(jnp.bfloat16)
    value_reduced_precision = grad_value.astype(jnp.bfloat16)
    grad_queries = query_low[:, actual_position_of].reshape(sequence_total, sequence_span_length, QUERY_HEADS * HEAD_SIZE)
    key_gradient_rows = key_reduced_precision[:, actual_position_of].reshape(sequence_total, sequence_span_length, KEY_VALUE_HEADS * HEAD_SIZE)
    value_gradient_rows = value_reduced_precision[:, actual_position_of].reshape(sequence_total, sequence_span_length, KEY_VALUE_HEADS * HEAD_SIZE)
    squares = jnp.sum(jnp.square(query_low.astype(jnp.float32))) + jnp.sum(jnp.square(key_reduced_precision.astype(jnp.float32))) + jnp.sum(jnp.square(value_reduced_precision.astype(jnp.float32)))
    return (grad_queries, key_gradient_rows, value_gradient_rows, jnp.sqrt(squares))
```

```python
import functools
import math

import jax
import jax.numpy as jnp
from jax import lax
from jax.experimental import pallas as pl
from jax.experimental.pallas import tpu as pltpu
from jax.sharding import PartitionSpec as P

HEAD_SIZE = 128
GROUP = 4
NEG_FILL = -1e30
SCALE = HEAD_SIZE**-0.5
LOG2E = math.log2(math.e)
NT = (((1,), (1,)), ((), ()))
NN = (((1,), (0,)), ((), ()))
TN = (((0,), (0,)), ((), ()))


def dot(a, b, dims):
    return lax.dot_general(a, b, dims, preferred_element_type=jnp.float32)


def attend_kernel(
    place, q_mine, q_theirs, g_mine, g_theirs, own, side, prev_same, prev_side,
    dq_mine, dq_theirs, own_grad, side_grad, prev_same_grad, prev_side_grad,
):
    core = place[0]
    rows = own.shape[1]
    half = rows // 2
    side_bias = jnp.where(place[1] == 1, 0.0, NEG_FILL)
    prev_bias = jnp.where(place[2] == 1, 0.0, NEG_FILL)
    biases = (None, side_bias, prev_bias, prev_bias)
    parts = (own, side, prev_same, prev_side)
    grads = (own_grad, side_grad, prev_same_grad, prev_side_grad)
    flip = core * half
    key_place = lax.broadcasted_iota(jnp.int32, (rows, rows), 0) ^ flip
    query_place = lax.broadcasted_iota(jnp.int32, (rows, rows), 1) ^ flip
    visible = key_place <= query_place
    key_sums = [None] * len(parts)
    value_sums = [None] * len(parts)
    for head in range(GROUP):
        cols = slice(head * HEAD_SIZE, (head + 1) * HEAD_SIZE)
        q = jnp.concatenate([q_mine[:, cols], q_theirs[:, cols]], axis=0)
        g = jnp.concatenate([g_mine[:, cols], g_theirs[:, cols]], axis=0)
        scores = [dot(part[0], q, NT) for part in parts]
        scores[0] = jnp.where(visible, scores[0], NEG_FILL)
        tops = [jnp.max(s, axis=0, keepdims=True) for s in scores]
        tops = [t if b is None else t + b for t, b in zip(tops, biases)]
        top = functools.reduce(jnp.maximum, tops) * (SCALE * LOG2E)
        expos = [
            jnp.exp2(s * (SCALE * LOG2E) - (top if b is None else top - b))
            for s, b in zip(scores, biases)
        ]
        total = sum(jnp.sum(e, axis=0, keepdims=True) for e in expos)
        inverse = 1.0 / total
        probs = [e * inverse for e in expos]
        dprobs = [dot(part[1], g, NT) for part in parts]
        delta = sum(jnp.sum(p * d, axis=0, keepdims=True) for p, d in zip(probs, dprobs))
        dq = None
        for i, part in enumerate(parts):
            ds = (probs[i] * (dprobs[i] - delta)).astype(jnp.bfloat16)
            low = probs[i].astype(jnp.bfloat16)
            dv = dot(low, g, NN)
            dk = dot(ds, q, NN)
            value_sums[i] = dv if head == 0 else value_sums[i] + dv
            key_sums[i] = dk if head == 0 else key_sums[i] + dk
            step = dot(ds, part[0], TN)
            dq = step if dq is None else dq + step
        dq = (dq * SCALE).astype(dq_mine.dtype)
        dq_mine[:, cols] = dq[:half]
        dq_theirs[:, cols] = dq[half:]
    for i, out in enumerate(grads):
        out[0] = (key_sums[i] * SCALE).astype(out.dtype)
        out[1] = value_sums[i].astype(out.dtype)


def attend(place, q, g, qg_theirs, own, side, prev_same, prev_side):
    rows = q.shape[0]
    wide = GROUP * HEAD_SIZE
    groups = own.shape[2] // HEAD_SIZE
    mine_spec = pl.BlockSpec((rows, wide), lambda j, p: (0, p[0] * groups + j))
    q_spec = pl.BlockSpec((rows, wide), lambda j, p: (0, j))
    g_spec = pl.BlockSpec((rows, wide), lambda j, p: (0, groups + j))
    kv_spec = pl.BlockSpec((2, own.shape[1], HEAD_SIZE), lambda j, p: (0, 0, j))
    dq_shape = jax.ShapeDtypeStruct((rows, groups * wide), q.dtype)
    return pl.pallas_call(
        attend_kernel,
        grid_spec=pltpu.PrefetchScalarGridSpec(
            num_scalar_prefetch=1,
            grid=(groups,),
            in_specs=[mine_spec, q_spec, mine_spec, g_spec] + [kv_spec] * 4,
            out_specs=[q_spec, q_spec] + [kv_spec] * 4,
        ),
        out_shape=[dq_shape, dq_shape, jax.ShapeDtypeStruct(own.shape, jnp.float32)]
        + [jax.ShapeDtypeStruct(own.shape, q.dtype)] * 3,
        compiler_params=pltpu.CompilerParams(vmem_limit_bytes=40 * 1024 * 1024),
        cost_estimate=pl.CostEstimate(
            flops=10 * 4 * own.shape[1] * 2 * rows * HEAD_SIZE * groups * GROUP,
            bytes_accessed=8 * 1024 * 1024,
            transcendentals=4 * own.shape[1] * 2 * rows * groups * GROUP,
        ),
    )(place, q, qg_theirs, g, qg_theirs, own, side, prev_same, prev_side)


def square_total(x):
    return jnp.sum(jnp.square(x.astype(jnp.float32)))


def body(queries, keys, values, output_gradient_stored):
    q, k, v, g = queries[0], keys[0], values[0], output_gradient_stored[0]
    contexts, heads = lax.axis_size("ctx"), lax.axis_size("head")
    quarter = heads // 2
    ctx, head = lax.axis_index("ctx"), lax.axis_index("head")
    core = head % 2
    is_back = head >= quarter
    place = jnp.stack(
        [core, (head // 2) % 2, jnp.where((ctx > 0) | is_back, 1, 0)]
    ).astype(jnp.int32)
    core_pairs = [(h, h ^ 1) for h in range(heads)]
    side_pairs = [(h, h ^ 2) for h in range(heads)]

    def flat(c, h):
        return c * heads + h

    chain = []
    for h in range(quarter):
        chain += [(flat(c, h), flat(c + 1, h)) for c in range(contexts - 1)]
        chain += [(flat(contexts - 1, h), flat(contexts - 1, h + quarter))]
        chain += [(flat(c, h + quarter), flat(c - 1, h + quarter)) for c in range(1, contexts)]
    back = [(target, source) for source, target in chain]

    def swap_core(x):
        return lax.ppermute(x, "head", core_pairs)

    def swap_side(x):
        return lax.ppermute(x, "head", side_pairs)

    def cut(x, which):
        width = x.shape[1] // 2
        return lax.dynamic_slice_in_dim(x, which * width, width, axis=1)

    kv_theirs = swap_core(jnp.stack([cut(k, 1 - core), cut(v, 1 - core)]))
    own = jnp.concatenate([jnp.stack([cut(k, core), cut(v, core)]), kv_theirs], axis=1)
    side = swap_side(own)
    prev_same = lax.ppermute(own, ("ctx", "head"), chain)
    qg_theirs = swap_core(jnp.concatenate([cut(q, 1 - core), cut(g, 1 - core)], axis=1))
    prev_side = lax.ppermute(side, ("ctx", "head"), chain)

    dq_mine, dq_theirs, own_grad, side_grad, prev_same_grad, prev_side_grad = attend(
        place, q, g, qg_theirs, own, side, prev_same, prev_side
    )
    next_side = lax.ppermute(prev_side_grad, ("ctx", "head"), back)
    next_same = lax.ppermute(prev_same_grad, ("ctx", "head"), back)
    dq_back = swap_core(dq_theirs)
    side_sum = (side_grad.astype(jnp.float32) + next_side.astype(jnp.float32)).astype(q.dtype)
    from_side = swap_side(side_sum)
    total = (own_grad + next_same.astype(jnp.float32) + from_side.astype(jnp.float32)).astype(
        q.dtype
    )
    rows = q.shape[0]
    total_back = swap_core(total[:, rows:])

    def join(mine, theirs):
        low = jnp.where(core == 0, mine, theirs)
        high = jnp.where(core == 0, theirs, mine)
        return jnp.concatenate([low, high], axis=-1)

    grad_kv = join(total[:, :rows], total_back)
    grad_q = join(dq_mine, dq_back)
    squares = square_total(dq_mine) + square_total(dq_theirs) + square_total(total)
    norm_square = lax.psum(squares, ("dp", "ctx", "head"))
    return (grad_q[None], grad_kv[0][None], grad_kv[1][None], jnp.sqrt(norm_square))


def solution(mesh):
    spec = P("dp", ("ctx", "head"), None)
    return jax.shard_map(
        body,
        mesh=mesh,
        in_specs=(spec, spec, spec, spec),
        out_specs=(spec, spec, spec, P()),
        check_vma=False,
    )
```

```python
import functools
import math

import jax
import jax.numpy as jnp
from jax import lax
from jax.experimental import pallas as pl
from jax.experimental.pallas import tpu as pltpu
from jax.sharding import PartitionSpec as P

HEAD_SIZE = 128
GROUP = 4
NEG_FILL = -1e30
SCALE = HEAD_SIZE**-0.5
RATE = SCALE * math.log2(math.e)
VMEM = 60 * 1024 * 1024
NT = (((1,), (1,)), ((), ()))
NN = (((1,), (0,)), ((), ()))
TN = (((0,), (0,)), ((), ()))


def dot(a, b, dims):
    return lax.dot_general(a, b, dims, preferred_element_type=jnp.float32)


def pair(mine, theirs, head):
    cols = slice(head * HEAD_SIZE, (head + 1) * HEAD_SIZE)
    return jnp.concatenate([mine[:, cols], theirs[:, cols]], axis=0)


def own_scores(place, keys, q):
    rows = keys.shape[0]
    flip = place[0] * (rows // 2)
    key_place = lax.broadcasted_iota(jnp.int32, (rows, rows), 0) ^ flip
    query_place = lax.broadcasted_iota(jnp.int32, (rows, rows), 1) ^ flip
    return jnp.where(key_place <= query_place, dot(keys, q, NT), NEG_FILL)


def own_kernel(place, q_mine, q_theirs, g_mine, g_theirs, own, stats):
    for head in range(GROUP):
        q = pair(q_mine, q_theirs, head)
        g = pair(g_mine, g_theirs, head)
        scores = own_scores(place, own[0], q)
        top = jnp.max(scores, axis=0, keepdims=True)
        expos = jnp.exp2(scores * RATE - top * RATE)
        dprobs = dot(own[1], g, NT)
        stats[0, head : head + 1] = top
        stats[0, GROUP + head : GROUP + head + 1] = jnp.sum(expos, axis=0, keepdims=True)
        stats[0, 2 * GROUP + head : 2 * GROUP + head + 1] = jnp.sum(
            expos * dprobs, axis=0, keepdims=True
        )


def remote_kernel(
    place, q_mine, q_theirs, g_mine, g_theirs, own_stats, cross, same, side,
    side_grad, same_grad, cross_grad, dscores, stats,
):
    side_bias = jnp.where(place[1] == 1, 0.0, NEG_FILL)
    prev_bias = jnp.where(place[2] == 1, 0.0, NEG_FILL)
    biases = (side_bias, prev_bias, prev_bias)
    parts = (side, same, cross)
    rows = side.shape[1]
    key_sums = [None] * len(parts)
    value_sums = [None] * len(parts)
    for head in range(GROUP):
        q = pair(q_mine, q_theirs, head)
        g = pair(g_mine, g_theirs, head)
        own_top = own_stats[0, head : head + 1]
        own_total = own_stats[0, GROUP + head : GROUP + head + 1]
        own_delta = own_stats[0, 2 * GROUP + head : 2 * GROUP + head + 1]
        scores = [dot(part[0], q, NT) for part in parts]
        tops = [jnp.max(s, axis=0, keepdims=True) + b for s, b in zip(scores, biases)]
        top = functools.reduce(jnp.maximum, tops + [own_top]) * RATE
        expos = [jnp.exp2(s * RATE - (top - b)) for s, b in zip(scores, biases)]
        weight = jnp.exp2(own_top * RATE - top)
        total = sum(jnp.sum(e, axis=0, keepdims=True) for e in expos) + own_total * weight
        inverse = 1.0 / total
        dprobs = [dot(part[1], g, NT) for part in parts]
        delta = sum(jnp.sum(e * d, axis=0, keepdims=True) for e, d in zip(expos, dprobs))
        delta = (delta + own_delta * weight) * inverse
        stats[0, head : head + 1] = top
        stats[0, GROUP + head : GROUP + head + 1] = inverse
        stats[0, 2 * GROUP + head : 2 * GROUP + head + 1] = delta
        for i in range(len(parts)):
            probs = expos[i] * inverse
            low = probs.astype(jnp.bfloat16)
            ds = (probs * (dprobs[i] - delta)).astype(jnp.bfloat16)
            dscores[0, head, i * rows : (i + 1) * rows] = ds
            dv = dot(low, g, NN)
            dk = dot(ds, q, NN)
            value_sums[i] = dv if head == 0 else value_sums[i] + dv
            key_sums[i] = dk if head == 0 else key_sums[i] + dk
    for i, out in enumerate((side_grad, same_grad, cross_grad)):
        out[0] = (key_sums[i] * SCALE).astype(out.dtype)
        out[1] = value_sums[i].astype(out.dtype)


def rest_kernel(
    place, q_mine, q_theirs, g_mine, g_theirs, stats, own, side, same, cross, dscores,
    dq_mine, dq_theirs, own_grad, squares,
):
    half = dq_mine.shape[0]
    rows = 2 * half
    key_sum = value_sum = None
    square = jnp.zeros((8, HEAD_SIZE), jnp.float32)
    for head in range(GROUP):
        q = pair(q_mine, q_theirs, head)
        g = pair(g_mine, g_theirs, head)
        top = stats[0, head : head + 1]
        inverse = stats[0, GROUP + head : GROUP + head + 1]
        delta = stats[0, 2 * GROUP + head : 2 * GROUP + head + 1]
        probs = jnp.exp2(own_scores(place, own[0], q) * RATE - top) * inverse
        low = probs.astype(jnp.bfloat16)
        ds = (probs * (dot(own[1], g, NT) - delta)).astype(jnp.bfloat16)
        dv = dot(low, g, NN)
        dk = dot(ds, q, NN)
        value_sum = dv if head == 0 else value_sum + dv
        key_sum = dk if head == 0 else key_sum + dk
        dq = dot(ds, own[0], TN)
        for i, part in enumerate((side, same, cross)):
            dq = dq + dot(dscores[0, head, i * rows : (i + 1) * rows], part[0], TN)
        dq = (dq * SCALE).astype(dq_mine.dtype)
        cols = slice(head * HEAD_SIZE, (head + 1) * HEAD_SIZE)
        dq_mine[:, cols] = dq[:half]
        dq_theirs[:, cols] = dq[half:]
        wide = dq.astype(jnp.float32)
        square = square + jnp.sum((wide * wide).reshape(rows // 8, 8, HEAD_SIZE), axis=0)
    own_grad[0] = key_sum * SCALE
    own_grad[1] = value_sum

    @pl.when(pl.program_id(0) == 0)
    def _():
        squares[...] = jnp.zeros_like(squares)

    squares[...] += square


def total_kernel(own, side, same, cross, dq_squares, mine, theirs, sums):
    total = own[...] + side[...].astype(jnp.float32)
    total = total + same[...].astype(jnp.float32) + cross[...].astype(jnp.float32)
    total = total.astype(mine.dtype)
    half = mine.shape[1]
    mine[...] = total[:, :half]
    theirs[...] = total[:, half:]
    wide = total.astype(jnp.float32)
    square = jnp.sum((wide * wide).reshape(-1, 8, wide.shape[-1]), axis=0)
    square = jnp.sum(square, keepdims=True) + jnp.sum(dq_squares[...], keepdims=True)
    sums[...] = jnp.broadcast_to(square, sums.shape)


def call(kernel, groups, ins, outs, flops, exps, *args):
    return pl.pallas_call(
        kernel,
        grid_spec=pltpu.PrefetchScalarGridSpec(
            num_scalar_prefetch=1,
            grid=(groups,),
            in_specs=ins,
            out_specs=[spec for spec, _ in outs],
        ),
        out_shape=[shape for _, shape in outs],
        compiler_params=pltpu.CompilerParams(vmem_limit_bytes=VMEM),
        cost_estimate=pl.CostEstimate(
            flops=flops, bytes_accessed=4 * 1024 * 1024, transcendentals=exps
        ),
    )(*args)


def all_sum(x, axes):
    given = lax.all_to_all(x, axes, 0, 0, tiled=True)
    return jnp.sum(given, axis=0, keepdims=True)


def body(queries, keys, values, output_gradient_stored):
    q, k, v, g = queries[0], keys[0], values[0], output_gradient_stored[0]
    contexts, heads = lax.axis_size("ctx"), lax.axis_size("head")
    quarter = heads // 2
    ctx, head = lax.axis_index("ctx"), lax.axis_index("head")
    core = head % 2
    is_back = head >= quarter
    place = jnp.stack(
        [core, (head // 2) % 2, jnp.where((ctx > 0) | is_back, 1, 0)]
    ).astype(jnp.int32)
    core_pairs = [(h, h ^ 1) for h in range(heads)]
    side_pairs = [(h, h ^ 2) for h in range(heads) if h & 2 == 0]
    side_back = [(target, source) for source, target in side_pairs]

    def flat(c, h):
        return c * heads + h

    chain = []
    for h in range(quarter):
        chain += [(flat(c, h), flat(c + 1, h)) for c in range(contexts - 1)]
        chain += [(flat(contexts - 1, h), flat(contexts - 1, h + quarter))]
        chain += [(flat(c, h + quarter), flat(c - 1, h + quarter)) for c in range(1, contexts)]
    slant = [(source, target ^ 2) for source, target in chain]
    chain_back = [(target, source) for source, target in chain]
    slant_back = [(target, source) for source, target in slant]
    both = ("ctx", "head")

    def swap_core(x):
        return lax.ppermute(x, "head", core_pairs)

    def cut(x, which):
        width = x.shape[1] // 2
        return lax.dynamic_slice_in_dim(x, which * width, width, axis=1)

    rows = q.shape[0]
    kv_theirs = swap_core(jnp.stack([cut(k, 1 - core), cut(v, 1 - core)]))
    own = jnp.concatenate([jnp.stack([cut(k, core), cut(v, core)]), kv_theirs], axis=1)
    side = lax.ppermute(own, "head", side_pairs)
    same = lax.ppermute(own, both, chain)
    cross = lax.ppermute(own, both, slant)
    qg_theirs = jnp.concatenate([cut(q, 1 - core), cut(g, 1 - core)], axis=1)
    qg_theirs, own_late = lax.optimization_barrier((qg_theirs, own))
    qg_theirs = swap_core(qg_theirs)

    groups = own.shape[2] // HEAD_SIZE
    wide = GROUP * HEAD_SIZE
    span = own.shape[1]
    mine_spec = pl.BlockSpec((rows, wide), lambda j, p: (0, p[0] * groups + j))
    q_spec = pl.BlockSpec((rows, wide), lambda j, p: (0, j))
    g_spec = pl.BlockSpec((rows, wide), lambda j, p: (0, groups + j))
    kv_spec = pl.BlockSpec((2, span, HEAD_SIZE), lambda j, p: (0, 0, j))
    k_spec = pl.BlockSpec((1, span, HEAD_SIZE), lambda j, p: (0, 0, j))
    stat_spec = pl.BlockSpec((1, 4 * GROUP, span), lambda j, p: (j, 0, 0))
    ds_spec = pl.BlockSpec((1, GROUP, 3 * span, span), lambda j, p: (j, 0, 0, 0))
    square_spec = pl.BlockSpec((8, HEAD_SIZE), lambda j, p: (0, 0))
    qg_specs = [mine_spec, q_spec, mine_spec, g_spec]
    stat = (stat_spec, jax.ShapeDtypeStruct((groups, 4 * GROUP, span), jnp.float32))
    grad = (kv_spec, jax.ShapeDtypeStruct(own.shape, q.dtype))
    part = (q_spec, jax.ShapeDtypeStruct((rows, groups * wide), q.dtype))
    unit = 2 * span * span * HEAD_SIZE * groups * GROUP
    exps = span * span * groups * GROUP
    rows_in = (place, q, qg_theirs, g, qg_theirs)

    (own_stats,) = call(
        own_kernel, groups, qg_specs + [kv_spec], [stat], 2 * unit, exps, *rows_in, own
    )
    side_grad, same_grad, cross_grad, dscores, stats = call(
        remote_kernel,
        groups,
        qg_specs + [stat_spec] + [kv_spec] * 3,
        [grad] * 3
        + [(ds_spec, jax.ShapeDtypeStruct((groups, GROUP, 3 * span, span), q.dtype)), stat],
        12 * unit,
        3 * exps,
        *rows_in, own_stats, cross, same, side,
    )
    from_side = lax.ppermute(side_grad, "head", side_back)
    next_same = lax.ppermute(same_grad, both, chain_back)
    next_cross = lax.ppermute(cross_grad, both, slant_back)
    dq_mine, dq_theirs, own_grad, dq_squares = call(
        rest_kernel,
        groups,
        qg_specs + [stat_spec, kv_spec] + [k_spec] * 3 + [ds_spec],
        [part, part, (kv_spec, jax.ShapeDtypeStruct(own.shape, jnp.float32))]
        + [(square_spec, jax.ShapeDtypeStruct((8, HEAD_SIZE), jnp.float32))],
        8 * unit,
        exps,
        *rows_in, stats, own, side, same, cross, dscores,
    )
    dq_back = swap_core(dq_theirs)
    near = lax.axis_size("head")
    half_shape = jax.ShapeDtypeStruct((2, rows, own.shape[2]), q.dtype)
    total_mine, total_theirs, sums = pl.pallas_call(
        total_kernel,
        out_shape=[half_shape, half_shape, jax.ShapeDtypeStruct((near, HEAD_SIZE), jnp.float32)],
        compiler_params=pltpu.CompilerParams(vmem_limit_bytes=24 * 1024 * 1024),
    )(own_grad, from_side, next_same, next_cross, dq_squares)

    def join(mine, theirs):
        low = jnp.where(core == 0, mine, theirs)
        high = jnp.where(core == 0, theirs, mine)
        return jnp.concatenate([low, high], axis=-1)

    grad_q = join(dq_mine, dq_back)
    sums = all_sum(sums, "head")
    grad_kv = join(total_mine, swap_core(total_theirs))
    norm_square = all_sum(jnp.broadcast_to(sums, (2 * contexts, HEAD_SIZE)), ("dp", "ctx"))[0, 0]
    return (grad_q[None], grad_kv[0][None], grad_kv[1][None], jnp.sqrt(norm_square))


def solution(mesh):
    spec = P("dp", ("ctx", "head"), None)
    return jax.shard_map(
        body,
        mesh=mesh,
        in_specs=(spec, spec, spec, spec),
        out_specs=(spec, spec, spec, P()),
        check_vma=False,
    )
```

```python
import functools
import math

import jax
import jax.numpy as jnp
from jax import lax
from jax.experimental import pallas as pl
from jax.experimental.pallas import tpu as pltpu
from jax.sharding import PartitionSpec as P

HEAD_SIZE = 128
GROUP = 4
NEG_FILL = -1e30
SCALE = HEAD_SIZE**-0.5
RATE = SCALE * math.log2(math.e)
VMEM = 60 * 1024 * 1024
NT = (((1,), (1,)), ((), ()))
NN = (((1,), (0,)), ((), ()))
TN = (((0,), (0,)), ((), ()))


def dot(a, b, dims):
    return lax.dot_general(a, b, dims, preferred_element_type=jnp.float32)


def pair(mine, theirs, head):
    cols = slice(head * HEAD_SIZE, (head + 1) * HEAD_SIZE)
    return jnp.concatenate([mine[:, cols], theirs[:, cols]], axis=0)


def own_scores(place, keys, q):
    rows = keys.shape[0]
    flip = place[0] * (rows // 2)
    key_place = lax.broadcasted_iota(jnp.int32, (rows, rows), 0) ^ flip
    query_place = lax.broadcasted_iota(jnp.int32, (rows, rows), 1) ^ flip
    return jnp.where(key_place <= query_place, dot(keys, q, NT), NEG_FILL)


def own_kernel(place, q_mine, q_theirs, g_mine, g_theirs, own, stats):
    for head in range(GROUP):
        q = pair(q_mine, q_theirs, head)
        g = pair(g_mine, g_theirs, head)
        scores = own_scores(place, own[0], q)
        top = jnp.max(scores, axis=0, keepdims=True)
        expos = jnp.exp2(scores * RATE - top * RATE)
        dprobs = dot(own[1], g, NT)
        stats[0, head : head + 1] = top
        stats[0, GROUP + head : GROUP + head + 1] = jnp.sum(expos, axis=0, keepdims=True)
        stats[0, 2 * GROUP + head : 2 * GROUP + head + 1] = jnp.sum(
            expos * dprobs, axis=0, keepdims=True
        )


def remote_kernel(
    place, q_mine, q_theirs, g_mine, g_theirs, own_stats, side, same, cross,
    side_grad, same_grad, cross_grad, dscores, stats,
):
    side_bias = jnp.where(place[1] == 1, 0.0, NEG_FILL)
    prev_bias = jnp.where(place[2] == 1, 0.0, NEG_FILL)
    biases = (side_bias, prev_bias, prev_bias)
    parts = (side, same, cross)
    rows = side.shape[1]
    key_sums = [None] * len(parts)
    value_sums = [None] * len(parts)
    for head in range(GROUP):
        q = pair(q_mine, q_theirs, head)
        g = pair(g_mine, g_theirs, head)
        own_top = own_stats[0, head : head + 1]
        own_total = own_stats[0, GROUP + head : GROUP + head + 1]
        own_delta = own_stats[0, 2 * GROUP + head : 2 * GROUP + head + 1]
        scores = [dot(part[0], q, NT) for part in parts]
        tops = [jnp.max(s, axis=0, keepdims=True) + b for s, b in zip(scores, biases)]
        top = functools.reduce(jnp.maximum, tops + [own_top]) * RATE
        expos = [jnp.exp2(s * RATE - (top - b)) for s, b in zip(scores, biases)]
        weight = jnp.exp2(own_top * RATE - top)
        total = sum(jnp.sum(e, axis=0, keepdims=True) for e in expos) + own_total * weight
        inverse = 1.0 / total
        dprobs = [dot(part[1], g, NT) for part in parts]
        delta = sum(jnp.sum(e * d, axis=0, keepdims=True) for e, d in zip(expos, dprobs))
        delta = (delta + own_delta * weight) * inverse
        stats[0, head : head + 1] = top
        stats[0, GROUP + head : GROUP + head + 1] = inverse
        stats[0, 2 * GROUP + head : 2 * GROUP + head + 1] = delta
        for i in range(len(parts)):
            probs = expos[i] * inverse
            low = probs.astype(jnp.bfloat16)
            ds = (probs * (dprobs[i] - delta)).astype(jnp.bfloat16)
            dscores[0, head, i * rows : (i + 1) * rows] = ds
            dv = dot(low, g, NN)
            dk = dot(ds, q, NN)
            value_sums[i] = dv if head == 0 else value_sums[i] + dv
            key_sums[i] = dk if head == 0 else key_sums[i] + dk
    for i, out in enumerate((side_grad, same_grad, cross_grad)):
        out[0] = (key_sums[i] * SCALE).astype(out.dtype)
        out[1] = value_sums[i].astype(out.dtype)


def rest_kernel(
    place, q_mine, q_theirs, g_mine, g_theirs, stats, own, side, same, cross, dscores,
    dq_mine, dq_theirs, own_grad, squares,
):
    half = dq_mine.shape[0]
    rows = 2 * half
    key_sum = value_sum = None
    square = jnp.zeros((8, HEAD_SIZE), jnp.float32)
    for head in range(GROUP):
        q = pair(q_mine, q_theirs, head)
        g = pair(g_mine, g_theirs, head)
        top = stats[0, head : head + 1]
        inverse = stats[0, GROUP + head : GROUP + head + 1]
        delta = stats[0, 2 * GROUP + head : 2 * GROUP + head + 1]
        probs = jnp.exp2(own_scores(place, own[0], q) * RATE - top) * inverse
        low = probs.astype(jnp.bfloat16)
        ds = (probs * (dot(own[1], g, NT) - delta)).astype(jnp.bfloat16)
        dv = dot(low, g, NN)
        dk = dot(ds, q, NN)
        value_sum = dv if head == 0 else value_sum + dv
        key_sum = dk if head == 0 else key_sum + dk
        dq = dot(ds, own[0], TN)
        for i, part in enumerate((side, same, cross)):
            dq = dq + dot(dscores[0, head, i * rows : (i + 1) * rows], part[0], TN)
        dq = (dq * SCALE).astype(dq_mine.dtype)
        cols = slice(head * HEAD_SIZE, (head + 1) * HEAD_SIZE)
        dq_mine[:, cols] = dq[:half]
        dq_theirs[:, cols] = dq[half:]
        wide = dq.astype(jnp.float32)
        square = square + jnp.sum((wide * wide).reshape(rows // 8, 8, HEAD_SIZE), axis=0)
    own_grad[0] = key_sum * SCALE
    own_grad[1] = value_sum

    @pl.when(pl.program_id(0) == 0)
    def _():
        squares[...] = jnp.zeros_like(squares)

    squares[...] += square


def total_kernel(near, same, cross, dq_squares, mine, theirs, sums):
    total = near[...] + same[...].astype(jnp.float32) + cross[...].astype(jnp.float32)
    total = total.astype(mine.dtype)
    half = mine.shape[1]
    mine[...] = total[:, :half]
    theirs[...] = total[:, half:]
    wide = total.astype(jnp.float32)
    square = jnp.sum((wide * wide).reshape(-1, 8, wide.shape[-1]), axis=0)
    square = jnp.sum(square, keepdims=True) + jnp.sum(dq_squares[...], keepdims=True)
    sums[...] = jnp.broadcast_to(square, sums.shape)


def call(kernel, groups, ins, outs, flops, exps, *args):
    return pl.pallas_call(
        kernel,
        grid_spec=pltpu.PrefetchScalarGridSpec(
            num_scalar_prefetch=1,
            grid=(groups,),
            in_specs=ins,
            out_specs=[spec for spec, _ in outs],
        ),
        out_shape=[shape for _, shape in outs],
        compiler_params=pltpu.CompilerParams(vmem_limit_bytes=VMEM),
        cost_estimate=pl.CostEstimate(
            flops=flops, bytes_accessed=4 * 1024 * 1024, transcendentals=exps
        ),
    )(*args)


def all_sum(x, axes):
    given = lax.all_to_all(x, axes, 0, 0, tiled=True)
    return jnp.sum(given, axis=0, keepdims=True)


def body(queries, keys, values, output_gradient_stored):
    q, k, v, g = queries[0], keys[0], values[0], output_gradient_stored[0]
    contexts, heads = lax.axis_size("ctx"), lax.axis_size("head")
    quarter = heads // 2
    ctx, head = lax.axis_index("ctx"), lax.axis_index("head")
    core = head % 2
    is_back = head >= quarter
    place = jnp.stack(
        [core, (head // 2) % 2, jnp.where((ctx > 0) | is_back, 1, 0)]
    ).astype(jnp.int32)
    core_pairs = [(h, h ^ 1) for h in range(heads)]
    side_pairs = [(h, h ^ 2) for h in range(heads) if h & 2 == 0]
    side_back = [(target, source) for source, target in side_pairs]

    def flat(c, h):
        return c * heads + h

    chain = []
    for h in range(quarter):
        chain += [(flat(c, h), flat(c + 1, h)) for c in range(contexts - 1)]
        chain += [(flat(contexts - 1, h), flat(contexts - 1, h + quarter))]
        chain += [(flat(c, h + quarter), flat(c - 1, h + quarter)) for c in range(1, contexts)]
    slant = [(source, target ^ 2) for source, target in chain]
    chain_back = [(target, source) for source, target in chain]
    slant_back = [(target, source) for source, target in slant]
    both = ("ctx", "head")

    def swap_core(x):
        return lax.ppermute(x, "head", core_pairs)

    def cut(x, which):
        width = x.shape[1] // 2
        return lax.dynamic_slice_in_dim(x, which * width, width, axis=1)

    rows = q.shape[0]
    kv_theirs = swap_core(jnp.stack([cut(k, 1 - core), cut(v, 1 - core)]))
    own = jnp.concatenate([jnp.stack([cut(k, core), cut(v, core)]), kv_theirs], axis=1)
    side = lax.ppermute(own, "head", side_pairs)
    same = lax.ppermute(own, both, chain)
    cross = lax.ppermute(own, both, slant)
    qg_theirs = jnp.concatenate([cut(q, 1 - core), cut(g, 1 - core)], axis=1)
    qg_theirs, own_late = lax.optimization_barrier((qg_theirs, own))
    qg_theirs = swap_core(qg_theirs)

    groups = own.shape[2] // HEAD_SIZE
    wide = GROUP * HEAD_SIZE
    span = own.shape[1]
    mine_spec = pl.BlockSpec((rows, wide), lambda j, p: (0, p[0] * groups + j))
    q_spec = pl.BlockSpec((rows, wide), lambda j, p: (0, j))
    g_spec = pl.BlockSpec((rows, wide), lambda j, p: (0, groups + j))
    kv_spec = pl.BlockSpec((2, span, HEAD_SIZE), lambda j, p: (0, 0, j))
    k_spec = pl.BlockSpec((1, span, HEAD_SIZE), lambda j, p: (0, 0, j))
    stat_spec = pl.BlockSpec((1, 4 * GROUP, span), lambda j, p: (j, 0, 0))
    ds_spec = pl.BlockSpec((1, GROUP, 3 * span, span), lambda j, p: (j, 0, 0, 0))
    square_spec = pl.BlockSpec((8, HEAD_SIZE), lambda j, p: (0, 0))
    qg_specs = [mine_spec, q_spec, mine_spec, g_spec]
    stat = (stat_spec, jax.ShapeDtypeStruct((groups, 4 * GROUP, span), jnp.float32))
    grad = (kv_spec, jax.ShapeDtypeStruct(own.shape, q.dtype))
    part = (q_spec, jax.ShapeDtypeStruct((rows, groups * wide), q.dtype))
    unit = 2 * span * span * HEAD_SIZE * groups * GROUP
    exps = span * span * groups * GROUP
    rows_in = (place, q, qg_theirs, g, qg_theirs)

    (own_stats,) = call(
        own_kernel, groups, qg_specs + [kv_spec], [stat], 2 * unit, exps, *rows_in, own
    )
    side_grad, same_grad, cross_grad, dscores, stats = call(
        remote_kernel,
        groups,
        qg_specs + [stat_spec] + [kv_spec] * 3,
        [grad] * 3
        + [(ds_spec, jax.ShapeDtypeStruct((groups, GROUP, 3 * span, span), q.dtype)), stat],
        12 * unit,
        3 * exps,
        *rows_in, own_stats, side, same, cross,
    )
    from_side = lax.ppermute(side_grad, "head", side_back)
    next_same = lax.ppermute(same_grad, both, chain_back)
    next_cross = lax.ppermute(cross_grad, both, slant_back)
    dq_mine, dq_theirs, own_grad, dq_squares = call(
        rest_kernel,
        groups,
        qg_specs + [stat_spec, kv_spec] + [k_spec] * 3 + [ds_spec],
        [part, part, (kv_spec, jax.ShapeDtypeStruct(own.shape, jnp.float32))]
        + [(square_spec, jax.ShapeDtypeStruct((8, HEAD_SIZE), jnp.float32))],
        8 * unit,
        exps,
        *rows_in, stats, own, side, same, cross, dscores,
    )
    dq_back = swap_core(dq_theirs)
    near = own_grad + from_side.astype(jnp.float32)
    dq_squares = jnp.sum(dq_squares, axis=0, keepdims=True)
    half_shape = jax.ShapeDtypeStruct((2, rows, own.shape[2]), q.dtype)
    total_mine, total_theirs, sums = pl.pallas_call(
        total_kernel,
        out_shape=[half_shape, half_shape, jax.ShapeDtypeStruct((heads, HEAD_SIZE), jnp.float32)],
        compiler_params=pltpu.CompilerParams(vmem_limit_bytes=24 * 1024 * 1024),
    )(near, next_same, next_cross, dq_squares)

    def join(mine, theirs):
        low = jnp.where(core == 0, mine, theirs)
        high = jnp.where(core == 0, theirs, mine)
        return jnp.concatenate([low, high], axis=-1)

    grad_q = join(dq_mine, dq_back)
    sums = all_sum(sums, "head")
    grad_kv = join(total_mine, swap_core(total_theirs))
    norm_square = all_sum(jnp.broadcast_to(sums, (2 * contexts, HEAD_SIZE)), ("dp", "ctx"))[0, 0]
    return (grad_q[None], grad_kv[0][None], grad_kv[1][None], jnp.sqrt(norm_square))


def solution(mesh):
    spec = P("dp", ("ctx", "head"), None)
    return jax.shard_map(
        body,
        mesh=mesh,
        in_specs=(spec, spec, spec, spec),
        out_specs=(spec, spec, spec, P()),
        check_vma=False,
    )
```

```python
import functools
import math

import jax
import jax.numpy as jnp
from jax import lax
from jax.experimental import pallas as pl
from jax.experimental.pallas import tpu as pltpu
from jax.sharding import PartitionSpec as P

HEAD_SIZE = 128
GROUP = 4
NEG_FILL = -1e30
SCALE = HEAD_SIZE**-0.5
RATE = SCALE * math.log2(math.e)
VMEM = 60 * 1024 * 1024
NT = (((1,), (1,)), ((), ()))
NN = (((1,), (0,)), ((), ()))
TN = (((0,), (0,)), ((), ()))


def dot(a, b, dims):
    return lax.dot_general(a, b, dims, preferred_element_type=jnp.float32)


def pair(mine, theirs, head):
    cols = slice(head * HEAD_SIZE, (head + 1) * HEAD_SIZE)
    return jnp.concatenate([mine[:, cols], theirs[:, cols]], axis=0)


def own_scores(place, keys, q):
    rows = keys.shape[0]
    flip = place[0] * (rows // 2)
    key_place = lax.broadcasted_iota(jnp.int32, (rows, rows), 0) ^ flip
    query_place = lax.broadcasted_iota(jnp.int32, (rows, rows), 1) ^ flip
    return jnp.where(key_place <= query_place, dot(keys, q, NT), NEG_FILL)


def own_kernel(place, q_mine, q_theirs, g_mine, g_theirs, own, stats):
    for head in range(GROUP):
        q = pair(q_mine, q_theirs, head)
        g = pair(g_mine, g_theirs, head)
        scores = own_scores(place, own[0], q)
        top = jnp.max(scores, axis=0, keepdims=True)
        expos = jnp.exp2(scores * RATE - top * RATE)
        dprobs = dot(own[1], g, NT)
        stats[0, head : head + 1] = top
        stats[0, GROUP + head : GROUP + head + 1] = jnp.sum(expos, axis=0, keepdims=True)
        stats[0, 2 * GROUP + head : 2 * GROUP + head + 1] = jnp.sum(
            expos * dprobs, axis=0, keepdims=True
        )


def remote_kernel(
    place, q_mine, q_theirs, g_mine, g_theirs, own_stats, side, same, cross, fold_same, fold_cross,
    side_grad, same_grad, cross_grad, dscores, stats,
):
    side_bias = jnp.where(place[1] == 1, 0.0, NEG_FILL)
    prev_bias = jnp.where(place[2] == 1, 0.0, NEG_FILL)
    biases = (side_bias, prev_bias, prev_bias)
    parts = [
        [part[i] if fold is None else part[i] + fold[i] for i in range(2)]
        for part, fold in ((side, None), (same, fold_same), (cross, fold_cross))
    ]
    rows = side.shape[1]
    key_sums = [None] * len(parts)
    value_sums = [None] * len(parts)
    for head in range(GROUP):
        q = pair(q_mine, q_theirs, head)
        g = pair(g_mine, g_theirs, head)
        own_top = own_stats[0, head : head + 1]
        own_total = own_stats[0, GROUP + head : GROUP + head + 1]
        own_delta = own_stats[0, 2 * GROUP + head : 2 * GROUP + head + 1]
        scores = [dot(part[0], q, NT) for part in parts]
        tops = [jnp.max(s, axis=0, keepdims=True) + b for s, b in zip(scores, biases)]
        top = functools.reduce(jnp.maximum, tops + [own_top]) * RATE
        expos = [jnp.exp2(s * RATE - (top - b)) for s, b in zip(scores, biases)]
        weight = jnp.exp2(own_top * RATE - top)
        total = sum(jnp.sum(e, axis=0, keepdims=True) for e in expos) + own_total * weight
        inverse = 1.0 / total
        dprobs = [dot(part[1], g, NT) for part in parts]
        delta = sum(jnp.sum(e * d, axis=0, keepdims=True) for e, d in zip(expos, dprobs))
        delta = (delta + own_delta * weight) * inverse
        stats[0, head : head + 1] = top
        stats[0, GROUP + head : GROUP + head + 1] = inverse
        stats[0, 2 * GROUP + head : 2 * GROUP + head + 1] = delta
        for i in range(len(parts)):
            probs = expos[i] * inverse
            low = probs.astype(jnp.bfloat16)
            ds = (probs * (dprobs[i] - delta)).astype(jnp.bfloat16)
            dscores[0, head, i * rows : (i + 1) * rows] = ds
            dv = dot(low, g, NN)
            dk = dot(ds, q, NN)
            value_sums[i] = dv if head == 0 else value_sums[i] + dv
            key_sums[i] = dk if head == 0 else key_sums[i] + dk
    for i, out in enumerate((side_grad, same_grad, cross_grad)):
        out[0] = (key_sums[i] * SCALE).astype(out.dtype)
        out[1] = value_sums[i].astype(out.dtype)


def rest_kernel(
    place, q_mine, q_theirs, g_mine, g_theirs, stats, own, side, same, cross, fold_same, fold_cross, dscores,
    dq_mine, dq_theirs, own_grad, squares,
):
    half = dq_mine.shape[0]
    rows = 2 * half
    key_sum = value_sum = None
    square = jnp.zeros((8, HEAD_SIZE), jnp.float32)
    keys = (side[0], same[0] + fold_same[0], cross[0] + fold_cross[0])
    for head in range(GROUP):
        q = pair(q_mine, q_theirs, head)
        g = pair(g_mine, g_theirs, head)
        top = stats[0, head : head + 1]
        inverse = stats[0, GROUP + head : GROUP + head + 1]
        delta = stats[0, 2 * GROUP + head : 2 * GROUP + head + 1]
        probs = jnp.exp2(own_scores(place, own[0], q) * RATE - top) * inverse
        low = probs.astype(jnp.bfloat16)
        ds = (probs * (dot(own[1], g, NT) - delta)).astype(jnp.bfloat16)
        dv = dot(low, g, NN)
        dk = dot(ds, q, NN)
        value_sum = dv if head == 0 else value_sum + dv
        key_sum = dk if head == 0 else key_sum + dk
        dq = dot(ds, own[0], TN)
        for i, key in enumerate(keys):
            dq = dq + dot(dscores[0, head, i * rows : (i + 1) * rows], key, TN)
        dq = (dq * SCALE).astype(dq_mine.dtype)
        cols = slice(head * HEAD_SIZE, (head + 1) * HEAD_SIZE)
        dq_mine[:, cols] = dq[:half]
        dq_theirs[:, cols] = dq[half:]
        wide = dq.astype(jnp.float32)
        square = square + jnp.sum((wide * wide).reshape(rows // 8, 8, HEAD_SIZE), axis=0)
    own_grad[0] = key_sum * SCALE
    own_grad[1] = value_sum

    @pl.when(pl.program_id(0) == 0)
    def _():
        squares[...] = jnp.zeros_like(squares)

    squares[...] += square


def total_kernel(near, same, cross, fold, dq_squares, mine, theirs, sums):
    total = near[...] + same[...].astype(jnp.float32) + cross[...].astype(jnp.float32)
    total = total + fold[...].astype(jnp.float32)
    total = total.astype(mine.dtype)
    half = mine.shape[1]
    mine[...] = total[:, :half]
    theirs[...] = total[:, half:]
    wide = total.astype(jnp.float32)
    square = jnp.sum((wide * wide).reshape(-1, 8, wide.shape[-1]), axis=0)
    square = jnp.sum(square, keepdims=True) + jnp.sum(dq_squares[...], keepdims=True)
    sums[...] = jnp.broadcast_to(square, sums.shape)


def call(kernel, groups, ins, outs, flops, exps, *args):
    return pl.pallas_call(
        kernel,
        grid_spec=pltpu.PrefetchScalarGridSpec(
            num_scalar_prefetch=1,
            grid=(groups,),
            in_specs=ins,
            out_specs=[spec for spec, _ in outs],
        ),
        out_shape=[shape for _, shape in outs],
        compiler_params=pltpu.CompilerParams(vmem_limit_bytes=VMEM),
        cost_estimate=pl.CostEstimate(
            flops=flops, bytes_accessed=4 * 1024 * 1024, transcendentals=exps
        ),
    )(*args)


def all_sum(x, axes):
    given = lax.all_to_all(x, axes, 0, 0, tiled=True)
    return jnp.sum(given, axis=0, keepdims=True)


def body(queries, keys, values, output_gradient_stored):
    q, k, v, g = queries[0], keys[0], values[0], output_gradient_stored[0]
    contexts, heads = lax.axis_size("ctx"), lax.axis_size("head")
    quarter = heads // 2
    ctx, head = lax.axis_index("ctx"), lax.axis_index("head")
    core = head % 2
    is_back = head >= quarter
    place = jnp.stack(
        [core, (head // 2) % 2, jnp.where((ctx > 0) | is_back, 1, 0)]
    ).astype(jnp.int32)
    core_pairs = [(h, h ^ 1) for h in range(heads)]
    side_pairs = [(h, h ^ 2) for h in range(heads) if h & 2 == 0]
    side_back = [(target, source) for source, target in side_pairs]

    def flat(c, h):
        return c * heads + h

    chain = []
    for h in range(quarter):
        chain += [(flat(c, h), flat(c + 1, h)) for c in range(contexts - 1)]
        chain += [(flat(c, h + quarter), flat(c - 1, h + quarter)) for c in range(1, contexts)]
    slant = [(source, target ^ 2) for source, target in chain]
    last = contexts - 1
    fold_far = [(flat(last, h), flat(last, (h + quarter) ^ 2)) for h in range(quarter)]
    fold_near = [(flat(last, h), flat(last, h ^ 2)) for h in range(quarter, heads)]
    fold_near_back = [(flat(last, h), flat(last, h ^ 2)) for h in range(quarter)]
    fold_far_back = [(target, source) for source, target in fold_far]
    chain_back = [(target, source) for source, target in chain]
    slant_back = [(target, source) for source, target in slant] + fold_far_back
    both = ("ctx", "head")

    def swap_core(x):
        return lax.ppermute(x, "head", core_pairs)

    def cut(x, which):
        width = x.shape[1] // 2
        return lax.dynamic_slice_in_dim(x, which * width, width, axis=1)

    rows = q.shape[0]
    kv_theirs = swap_core(jnp.stack([cut(k, 1 - core), cut(v, 1 - core)]))
    own = jnp.concatenate([jnp.stack([cut(k, core), cut(v, core)]), kv_theirs], axis=1)
    fold_cross = lax.ppermute(own, both, fold_far)
    side = lax.ppermute(own, "head", side_pairs)
    same = lax.ppermute(own, both, chain)
    cross = lax.ppermute(own, both, slant)
    qg_theirs = jnp.concatenate([cut(q, 1 - core), cut(g, 1 - core)], axis=1)
    qg_theirs, own_late = lax.optimization_barrier((qg_theirs, own))
    qg_theirs = swap_core(qg_theirs)

    groups = own.shape[2] // HEAD_SIZE
    wide = GROUP * HEAD_SIZE
    span = own.shape[1]
    mine_spec = pl.BlockSpec((rows, wide), lambda j, p: (0, p[0] * groups + j))
    q_spec = pl.BlockSpec((rows, wide), lambda j, p: (0, j))
    g_spec = pl.BlockSpec((rows, wide), lambda j, p: (0, groups + j))
    kv_spec = pl.BlockSpec((2, span, HEAD_SIZE), lambda j, p: (0, 0, j))
    k_spec = pl.BlockSpec((1, span, HEAD_SIZE), lambda j, p: (0, 0, j))
    stat_spec = pl.BlockSpec((1, 4 * GROUP, span), lambda j, p: (j, 0, 0))
    ds_spec = pl.BlockSpec((1, GROUP, 3 * span, span), lambda j, p: (j, 0, 0, 0))
    square_spec = pl.BlockSpec((8, HEAD_SIZE), lambda j, p: (0, 0))
    qg_specs = [mine_spec, q_spec, mine_spec, g_spec]
    stat = (stat_spec, jax.ShapeDtypeStruct((groups, 4 * GROUP, span), jnp.float32))
    grad = (kv_spec, jax.ShapeDtypeStruct(own.shape, q.dtype))
    part = (q_spec, jax.ShapeDtypeStruct((rows, groups * wide), q.dtype))
    unit = 2 * span * span * HEAD_SIZE * groups * GROUP
    exps = span * span * groups * GROUP
    rows_in = (place, q, qg_theirs, g, qg_theirs)

    (own_stats,) = call(
        own_kernel, groups, qg_specs + [kv_spec], [stat], 2 * unit, exps, *rows_in, own
    )
    fold_first, own_stats = lax.optimization_barrier((fold_cross, own_stats))
    fold_same = lax.ppermute(fold_first, both, fold_near)
    side_grad, same_grad, cross_grad, dscores, stats = call(
        remote_kernel,
        groups,
        qg_specs + [stat_spec] + [kv_spec] * 5,
        [grad] * 3
        + [(ds_spec, jax.ShapeDtypeStruct((groups, GROUP, 3 * span, span), q.dtype)), stat],
        12 * unit,
        3 * exps,
        *rows_in, own_stats, side, same, cross, fold_same, fold_cross,
    )
    fold_grad = lax.ppermute(same_grad, both, fold_far_back)
    from_side = lax.ppermute(side_grad, "head", side_back)
    next_same = lax.ppermute(same_grad, both, chain_back)
    next_cross = lax.ppermute(cross_grad, both, slant_back)
    dq_mine, dq_theirs, own_grad, dq_squares = call(
        rest_kernel,
        groups,
        qg_specs + [stat_spec, kv_spec] + [k_spec] * 5 + [ds_spec],
        [part, part, (kv_spec, jax.ShapeDtypeStruct(own.shape, jnp.float32))]
        + [(square_spec, jax.ShapeDtypeStruct((8, HEAD_SIZE), jnp.float32))],
        8 * unit,
        exps,
        *rows_in, stats, own, side, same, cross, fold_same, fold_cross, dscores,
    )
    fold_grad, dq_squares = lax.optimization_barrier((fold_grad, dq_squares))
    from_fold = lax.ppermute(fold_grad, both, fold_near_back)
    dq_back = swap_core(dq_theirs)
    near = own_grad + from_side.astype(jnp.float32)
    dq_squares = jnp.sum(dq_squares, axis=0, keepdims=True)
    half_shape = jax.ShapeDtypeStruct((2, rows, own.shape[2]), q.dtype)
    total_mine, total_theirs, sums = pl.pallas_call(
        total_kernel,
        out_shape=[half_shape, half_shape, jax.ShapeDtypeStruct((heads, HEAD_SIZE), jnp.float32)],
        compiler_params=pltpu.CompilerParams(vmem_limit_bytes=24 * 1024 * 1024),
    )(near, next_same, next_cross, from_fold, dq_squares)

    def join(mine, theirs):
        low = jnp.where(core == 0, mine, theirs)
        high = jnp.where(core == 0, theirs, mine)
        return jnp.concatenate([low, high], axis=-1)

    grad_q = join(dq_mine, dq_back)
    sums = all_sum(sums, "head")
    grad_kv = join(total_mine, swap_core(total_theirs))
    norm_square = all_sum(jnp.broadcast_to(sums, (2 * contexts, HEAD_SIZE)), ("dp", "ctx"))[0, 0]
    return (grad_q[None], grad_kv[0][None], grad_kv[1][None], jnp.sqrt(norm_square))


def solution(mesh):
    spec = P("dp", ("ctx", "head"), None)
    return jax.shard_map(
        body,
        mesh=mesh,
        in_specs=(spec, spec, spec, spec),
        out_specs=(spec, spec, spec, P()),
        check_vma=False,
    )
```

```python
import functools
import math

import jax
import jax.numpy as jnp
from jax import lax
from jax.experimental import pallas as pl
from jax.experimental.pallas import tpu as pltpu
from jax.sharding import PartitionSpec as P

HEAD_SIZE = 128
GROUP = 4
NEG_FILL = -1e30
SCALE = HEAD_SIZE**-0.5
RATE = SCALE * math.log2(math.e)
VMEM = 63 * 1024 * 1024
NT = (((1,), (1,)), ((), ()))
NN = (((1,), (0,)), ((), ()))
TN = (((0,), (0,)), ((), ()))


def dot(a, b, dims):
    return lax.dot_general(a, b, dims, preferred_element_type=jnp.float32)


def pair(mine, theirs, head):
    cols = slice(head * HEAD_SIZE, (head + 1) * HEAD_SIZE)
    return jnp.concatenate([mine[:, cols], theirs[:, cols]], axis=0)


def own_scores(place, keys, q):
    rows = keys.shape[0]
    flip = place[0] * (rows // 2)
    key_place = lax.broadcasted_iota(jnp.int32, (rows, rows), 0) ^ flip
    query_place = lax.broadcasted_iota(jnp.int32, (rows, rows), 1) ^ flip
    return jnp.where(key_place <= query_place, dot(keys, q, NT), NEG_FILL)


def own_kernel(place, q_mine, q_theirs, g_mine, g_theirs, own, stats):
    for head in range(GROUP):
        q = pair(q_mine, q_theirs, head)
        g = pair(g_mine, g_theirs, head)
        scores = own_scores(place, own[0], q)
        top = jnp.max(scores, axis=0, keepdims=True)
        expos = jnp.exp2(scores * RATE - top * RATE)
        dprobs = dot(own[1], g, NT)
        stats[0, head : head + 1] = top
        stats[0, GROUP + head : GROUP + head + 1] = jnp.sum(expos, axis=0, keepdims=True)
        stats[0, 2 * GROUP + head : 2 * GROUP + head + 1] = jnp.sum(
            expos * dprobs, axis=0, keepdims=True
        )


def remote_kernel(
    place, q_mine, q_theirs, g_mine, g_theirs, own_stats, side, same, cross, fold_same, fold_cross,
    side_grad, same_grad, cross_grad, dscores, stats,
):
    side_bias = jnp.where(place[1] == 1, 0.0, NEG_FILL)
    prev_bias = jnp.where(place[2] == 1, 0.0, NEG_FILL)
    biases = (side_bias, prev_bias, prev_bias)
    parts = [
        [part[i] if fold is None else part[i] + fold[i] for i in range(2)]
        for part, fold in ((side, None), (same, fold_same), (cross, fold_cross))
    ]
    rows = side.shape[1]
    key_sums = [None] * len(parts)
    value_sums = [None] * len(parts)
    for head in range(GROUP):
        q = pair(q_mine, q_theirs, head)
        g = pair(g_mine, g_theirs, head)
        own_top = own_stats[0, head : head + 1]
        own_total = own_stats[0, GROUP + head : GROUP + head + 1]
        own_delta = own_stats[0, 2 * GROUP + head : 2 * GROUP + head + 1]
        scores = [dot(part[0], q, NT) for part in parts]
        tops = [jnp.max(s, axis=0, keepdims=True) + b for s, b in zip(scores, biases)]
        top = functools.reduce(jnp.maximum, tops + [own_top]) * RATE
        expos = [jnp.exp2(s * RATE - (top - b)) for s, b in zip(scores, biases)]
        weight = jnp.exp2(own_top * RATE - top)
        total = sum(jnp.sum(e, axis=0, keepdims=True) for e in expos) + own_total * weight
        inverse = 1.0 / total
        dprobs = [dot(part[1], g, NT) for part in parts]
        delta = sum(jnp.sum(e * d, axis=0, keepdims=True) for e, d in zip(expos, dprobs))
        delta = (delta + own_delta * weight) * inverse
        stats[0, head : head + 1] = top
        stats[0, GROUP + head : GROUP + head + 1] = inverse
        stats[0, 2 * GROUP + head : 2 * GROUP + head + 1] = delta
        for i in range(len(parts)):
            probs = expos[i] * inverse
            low = probs.astype(jnp.bfloat16)
            ds = (probs * (dprobs[i] - delta)).astype(jnp.bfloat16)
            dscores[0, head, i * rows : (i + 1) * rows] = ds
            dv = dot(low, g, NN)
            dk = dot(ds, q, NN)
            value_sums[i] = dv if head == 0 else value_sums[i] + dv
            key_sums[i] = dk if head == 0 else key_sums[i] + dk
    for i, out in enumerate((side_grad, same_grad, cross_grad)):
        out[0] = (key_sums[i] * SCALE).astype(out.dtype)
        out[1] = value_sums[i].astype(out.dtype)


def rest_kernel(
    place, q_mine, q_theirs, g_mine, g_theirs, stats, own, side, same, cross, fold_same, fold_cross, dscores,
    dq_mine, dq_theirs, own_grad, squares,
):
    half = dq_mine.shape[0]
    rows = 2 * half
    key_sum = value_sum = None
    square = jnp.zeros((8, HEAD_SIZE), jnp.float32)
    keys = (side[0], same[0] + fold_same[0], cross[0] + fold_cross[0])
    for head in range(GROUP):
        q = pair(q_mine, q_theirs, head)
        g = pair(g_mine, g_theirs, head)
        top = stats[0, head : head + 1]
        inverse = stats[0, GROUP + head : GROUP + head + 1]
        delta = stats[0, 2 * GROUP + head : 2 * GROUP + head + 1]
        probs = jnp.exp2(own_scores(place, own[0], q) * RATE - top) * inverse
        low = probs.astype(jnp.bfloat16)
        ds = (probs * (dot(own[1], g, NT) - delta)).astype(jnp.bfloat16)
        dv = dot(low, g, NN)
        dk = dot(ds, q, NN)
        value_sum = dv if head == 0 else value_sum + dv
        key_sum = dk if head == 0 else key_sum + dk
        dq = dot(ds, own[0], TN)
        for i, key in enumerate(keys):
            dq = dq + dot(dscores[0, head, i * rows : (i + 1) * rows], key, TN)
        dq = (dq * SCALE).astype(dq_mine.dtype)
        cols = slice(head * HEAD_SIZE, (head + 1) * HEAD_SIZE)
        dq_mine[:, cols] = dq[:half]
        dq_theirs[:, cols] = dq[half:]
        wide = dq.astype(jnp.float32)
        square = square + jnp.sum((wide * wide).reshape(rows // 8, 8, HEAD_SIZE), axis=0)
    own_grad[0] = key_sum * SCALE
    own_grad[1] = value_sum

    @pl.when(pl.program_id(0) == 0)
    def _():
        squares[...] = jnp.zeros_like(squares)

    squares[...] += square


def total_kernel(near, same, cross, fold, dq_squares, mine, theirs, sums):
    total = near[...] + same[...].astype(jnp.float32) + cross[...].astype(jnp.float32)
    total = total + fold[...].astype(jnp.float32)
    total = total.astype(mine.dtype)
    half = mine.shape[1]
    mine[...] = total[:, :half]
    theirs[...] = total[:, half:]
    wide = total.astype(jnp.float32)
    square = jnp.sum((wide * wide).reshape(-1, 8, wide.shape[-1]), axis=0)
    square = jnp.sum(square, keepdims=True) + jnp.sum(dq_squares[...], keepdims=True)
    sums[...] = jnp.broadcast_to(square, sums.shape)


def call(kernel, groups, ins, outs, flops, exps, *args):
    return pl.pallas_call(
        kernel,
        grid_spec=pltpu.PrefetchScalarGridSpec(
            num_scalar_prefetch=1,
            grid=(groups,),
            in_specs=ins,
            out_specs=[spec for spec, _ in outs],
        ),
        out_shape=[shape for _, shape in outs],
        compiler_params=pltpu.CompilerParams(vmem_limit_bytes=VMEM),
        cost_estimate=pl.CostEstimate(
            flops=flops, bytes_accessed=4 * 1024 * 1024, transcendentals=exps
        ),
    )(*args)


def all_sum(x, axes):
    given = lax.all_to_all(x, axes, 0, 0, tiled=True)
    return jnp.sum(given, axis=0, keepdims=True)


def body(queries, keys, values, output_gradient_stored):
    q, k, v, g = queries[0], keys[0], values[0], output_gradient_stored[0]
    contexts, heads = lax.axis_size("ctx"), lax.axis_size("head")
    quarter = heads // 2
    ctx, head = lax.axis_index("ctx"), lax.axis_index("head")
    core = head % 2
    core_pairs = [(h, h ^ 1) for h in range(heads)]
    side_pairs = [(h, h ^ 2) for h in range(heads) if h & 2 == 0]
    side_back = [(target, source) for source, target in side_pairs]

    def flat(c, h):
        return c * heads + h

    chain = []
    for h in range(quarter):
        chain += [(flat(c, h), flat(c + 1, h)) for c in range(contexts - 1)]
        chain += [(flat(c, h + quarter), flat(c - 1, h + quarter)) for c in range(1, contexts)]
    slant = [(source, target ^ 2) for source, target in chain]
    last = contexts - 1
    fold_far = [(flat(last, h), flat(last, (h + quarter) ^ 2)) for h in range(quarter)]
    fold_near = [(flat(last, h), flat(last, h ^ 2)) for h in range(quarter, heads)]
    fold_near_back = [(flat(last, h), flat(last, h ^ 2)) for h in range(quarter)]
    fold_far_back = [(target, source) for source, target in fold_far]
    chain_back = [(target, source) for source, target in chain]
    slant_back = [(target, source) for source, target in slant] + fold_far_back
    both = ("ctx", "head")

    def swap_core(x):
        return lax.ppermute(x, "head", core_pairs)

    def cut(x, which):
        width = x.shape[1] // 2
        return lax.dynamic_slice_in_dim(x, which * width, width, axis=1)

    rows = q.shape[0]
    kv_theirs = swap_core(jnp.stack([cut(k, 1 - core), cut(v, 1 - core)]))
    own = jnp.concatenate([jnp.stack([cut(k, core), cut(v, core)]), kv_theirs], axis=1)
    fold_cross = lax.ppermute(own, both, fold_far)
    side = lax.ppermute(own, "head", side_pairs)
    same = lax.ppermute(own, both, chain)
    cross = lax.ppermute(own, both, slant)
    qg_theirs = jnp.concatenate([cut(q, 1 - core), cut(g, 1 - core)], axis=1)
    qg_theirs, own_late = lax.optimization_barrier((qg_theirs, own))
    qg_theirs = swap_core(qg_theirs)
    late_head, qg_theirs = lax.optimization_barrier((head, qg_theirs))
    place = jnp.stack(
        [late_head % 2, (late_head // 2) % 2, jnp.where((ctx > 0) | (late_head >= quarter), 1, 0)]
    ).astype(jnp.int32)

    groups = own.shape[2] // HEAD_SIZE
    wide = GROUP * HEAD_SIZE
    span = own.shape[1]
    mine_spec = pl.BlockSpec((rows, wide), lambda j, p: (0, p[0] * groups + j))
    q_spec = pl.BlockSpec((rows, wide), lambda j, p: (0, j))
    g_spec = pl.BlockSpec((rows, wide), lambda j, p: (0, groups + j))
    kv_spec = pl.BlockSpec((2, span, HEAD_SIZE), lambda j, p: (0, 0, j))
    k_spec = pl.BlockSpec((1, span, HEAD_SIZE), lambda j, p: (0, 0, j))
    stat_spec = pl.BlockSpec((1, 4 * GROUP, span), lambda j, p: (j, 0, 0))
    ds_spec = pl.BlockSpec((1, GROUP, 3 * span, span), lambda j, p: (j, 0, 0, 0))
    square_spec = pl.BlockSpec((8, HEAD_SIZE), lambda j, p: (0, 0))
    qg_specs = [mine_spec, q_spec, mine_spec, g_spec]
    stat = (stat_spec, jax.ShapeDtypeStruct((groups, 4 * GROUP, span), jnp.float32))
    grad = (kv_spec, jax.ShapeDtypeStruct(own.shape, q.dtype))
    part = (q_spec, jax.ShapeDtypeStruct((rows, groups * wide), q.dtype))
    unit = 2 * span * span * HEAD_SIZE * groups * GROUP
    exps = span * span * groups * GROUP
    rows_in = (place, q, qg_theirs, g, qg_theirs)

    (own_stats,) = call(
        own_kernel, groups, qg_specs + [kv_spec], [stat], 2 * unit, exps, *rows_in, own
    )
    fold_first, own_stats = lax.optimization_barrier((fold_cross, own_stats))
    fold_same = lax.ppermute(fold_first, both, fold_near)
    side_grad, same_grad, cross_grad, dscores, stats = call(
        remote_kernel,
        groups,
        qg_specs + [stat_spec] + [kv_spec] * 5,
        [grad] * 3
        + [(ds_spec, jax.ShapeDtypeStruct((groups, GROUP, 3 * span, span), q.dtype)), stat],
        12 * unit,
        3 * exps,
        *rows_in, own_stats, side, same, cross, fold_same, fold_cross,
    )
    fold_grad = lax.ppermute(same_grad, both, fold_far_back)
    from_side = lax.ppermute(side_grad, "head", side_back)
    next_same = lax.ppermute(same_grad, both, chain_back)
    next_cross = lax.ppermute(cross_grad, both, slant_back)
    dq_mine, dq_theirs, own_grad, dq_squares = call(
        rest_kernel,
        groups,
        qg_specs + [stat_spec, kv_spec] + [k_spec] * 5 + [ds_spec],
        [part, part, (kv_spec, jax.ShapeDtypeStruct(own.shape, jnp.float32))]
        + [(square_spec, jax.ShapeDtypeStruct((8, HEAD_SIZE), jnp.float32))],
        8 * unit,
        exps,
        *rows_in, stats, own, side, same, cross, fold_same, fold_cross, dscores,
    )
    fold_grad, dq_squares = lax.optimization_barrier((fold_grad, dq_squares))
    from_fold = lax.ppermute(fold_grad, both, fold_near_back)
    dq_back = swap_core(dq_theirs)
    near = own_grad + from_side.astype(jnp.float32)
    dq_squares = jnp.sum(dq_squares, axis=0, keepdims=True)
    half_shape = jax.ShapeDtypeStruct((2, rows, own.shape[2]), q.dtype)
    total_mine, total_theirs, sums = pl.pallas_call(
        total_kernel,
        out_shape=[half_shape, half_shape, jax.ShapeDtypeStruct((heads, HEAD_SIZE), jnp.float32)],
        compiler_params=pltpu.CompilerParams(vmem_limit_bytes=24 * 1024 * 1024),
    )(near, next_same, next_cross, from_fold, dq_squares)

    def join(mine, theirs):
        low = jnp.where(core == 0, mine, theirs)
        high = jnp.where(core == 0, theirs, mine)
        return jnp.concatenate([low, high], axis=-1)

    grad_q = join(dq_mine, dq_back)
    sums = all_sum(sums, "head")
    grad_kv = join(total_mine, swap_core(total_theirs))
    norm_square = all_sum(jnp.broadcast_to(sums, (2 * contexts, HEAD_SIZE)), ("dp", "ctx"))[0, 0]
    return (grad_q[None], grad_kv[0][None], grad_kv[1][None], jnp.sqrt(norm_square))


def solution(mesh):
    spec = P("dp", ("ctx", "head"), None)
    return jax.shard_map(
        body,
        mesh=mesh,
        in_specs=(spec, spec, spec, spec),
        out_specs=(spec, spec, spec, P()),
        check_vma=False,
    )
```

```python
import functools
import math

import jax
import jax.numpy as jnp
from jax import lax
from jax.experimental import pallas as pl
from jax.experimental.pallas import tpu as pltpu
from jax.sharding import PartitionSpec as P

HEAD_SIZE = 128
GROUP = 4
NEG_FILL = -1e30
SCALE = HEAD_SIZE**-0.5
RATE = SCALE * math.log2(math.e)
VMEM = 63 * 1024 * 1024
NT = (((1,), (1,)), ((), ()))
NN = (((1,), (0,)), ((), ()))
TN = (((0,), (0,)), ((), ()))


def dot(a, b, dims):
    return lax.dot_general(a, b, dims, preferred_element_type=jnp.float32)


def pair(mine, theirs, head):
    cols = slice(head * HEAD_SIZE, (head + 1) * HEAD_SIZE)
    return jnp.concatenate([mine[:, cols], theirs[:, cols]], axis=0)


def own_scores(place, keys, q):
    rows = keys.shape[0]
    flip = place[0] * (rows // 2)
    key_place = lax.broadcasted_iota(jnp.int32, (rows, rows), 0) ^ flip
    query_place = lax.broadcasted_iota(jnp.int32, (rows, rows), 1) ^ flip
    return jnp.where(key_place <= query_place, dot(keys, q, NT), NEG_FILL)


def own_kernel(place, q_mine, q_theirs, g_mine, g_theirs, own, stats):
    for head in range(GROUP):
        q = pair(q_mine, q_theirs, head)
        g = pair(g_mine, g_theirs, head)
        scores = own_scores(place, own[0], q)
        top = jnp.max(scores, axis=0, keepdims=True)
        expos = jnp.exp2(scores * RATE - top * RATE)
        dprobs = dot(own[1], g, NT)
        stats[0, head : head + 1] = top
        stats[0, GROUP + head : GROUP + head + 1] = jnp.sum(expos, axis=0, keepdims=True)
        stats[0, 2 * GROUP + head : 2 * GROUP + head + 1] = jnp.sum(
            expos * dprobs, axis=0, keepdims=True
        )


def remote_kernel(
    place, q_mine, q_theirs, g_mine, g_theirs, own_stats, side, same, cross, fold_same, fold_cross,
    side_grad, same_grad, cross_grad, dscores, stats,
):
    side_bias = jnp.where(place[1] == 1, 0.0, NEG_FILL)
    prev_bias = jnp.where(place[2] == 1, 0.0, NEG_FILL)
    biases = (side_bias, prev_bias, prev_bias)
    parts = [
        [part[i] if fold is None else part[i] + fold[i] for i in range(2)]
        for part, fold in ((side, None), (same, fold_same), (cross, fold_cross))
    ]
    rows = side.shape[1]
    key_sums = [None] * len(parts)
    value_sums = [None] * len(parts)
    for head in range(GROUP):
        q = pair(q_mine, q_theirs, head)
        g = pair(g_mine, g_theirs, head)
        own_top = own_stats[0, head : head + 1]
        own_total = own_stats[0, GROUP + head : GROUP + head + 1]
        own_delta = own_stats[0, 2 * GROUP + head : 2 * GROUP + head + 1]
        scores = [dot(part[0], q, NT) for part in parts]
        tops = [jnp.max(s, axis=0, keepdims=True) + b for s, b in zip(scores, biases)]
        top = functools.reduce(jnp.maximum, tops + [own_top]) * RATE
        expos = [jnp.exp2(s * RATE - (top - b)) for s, b in zip(scores, biases)]
        weight = jnp.exp2(own_top * RATE - top)
        total = sum(jnp.sum(e, axis=0, keepdims=True) for e in expos) + own_total * weight
        inverse = 1.0 / total
        dprobs = [dot(part[1], g, NT) for part in parts]
        delta = sum(jnp.sum(e * d, axis=0, keepdims=True) for e, d in zip(expos, dprobs))
        delta = (delta + own_delta * weight) * inverse
        stats[0, head : head + 1] = top
        stats[0, GROUP + head : GROUP + head + 1] = inverse
        stats[0, 2 * GROUP + head : 2 * GROUP + head + 1] = delta
        for i in range(len(parts)):
            probs = expos[i] * inverse
            low = probs.astype(jnp.bfloat16)
            ds = (probs * (dprobs[i] - delta)).astype(jnp.bfloat16)
            dscores[0, head, i * rows : (i + 1) * rows] = ds
            dv = dot(low, g, NN)
            dk = dot(ds, q, NN)
            value_sums[i] = dv if head == 0 else value_sums[i] + dv
            key_sums[i] = dk if head == 0 else key_sums[i] + dk
    for i, out in enumerate((side_grad, same_grad, cross_grad)):
        out[0] = (key_sums[i] * SCALE).astype(out.dtype)
        out[1] = value_sums[i].astype(out.dtype)


def rest_kernel(
    place, q_mine, q_theirs, g_mine, g_theirs, stats, own, side, same, cross, fold_same, fold_cross, dscores,
    dq_mine, dq_theirs, own_grad, squares,
):
    half = dq_mine.shape[0]
    rows = 2 * half
    key_sum = value_sum = None
    square = jnp.zeros((8, HEAD_SIZE), jnp.float32)
    keys = (side[0], same[0] + fold_same[0], cross[0] + fold_cross[0])
    for head in range(GROUP):
        q = pair(q_mine, q_theirs, head)
        g = pair(g_mine, g_theirs, head)
        top = stats[0, head : head + 1]
        inverse = stats[0, GROUP + head : GROUP + head + 1]
        delta = stats[0, 2 * GROUP + head : 2 * GROUP + head + 1]
        probs = jnp.exp2(own_scores(place, own[0], q) * RATE - top) * inverse
        low = probs.astype(jnp.bfloat16)
        ds = (probs * (dot(own[1], g, NT) - delta)).astype(jnp.bfloat16)
        dv = dot(low, g, NN)
        dk = dot(ds, q, NN)
        value_sum = dv if head == 0 else value_sum + dv
        key_sum = dk if head == 0 else key_sum + dk
        dq = dot(ds, own[0], TN)
        for i, key in enumerate(keys):
            dq = dq + dot(dscores[0, head, i * rows : (i + 1) * rows], key, TN)
        dq = (dq * SCALE).astype(dq_mine.dtype)
        cols = slice(head * HEAD_SIZE, (head + 1) * HEAD_SIZE)
        dq_mine[:, cols] = dq[:half]
        dq_theirs[:, cols] = dq[half:]
        wide = dq.astype(jnp.float32)
        square = square + jnp.sum((wide * wide).reshape(rows // 8, 8, HEAD_SIZE), axis=0)
    own_grad[0] = key_sum * SCALE
    own_grad[1] = value_sum

    @pl.when(pl.program_id(0) == 0)
    def _():
        squares[...] = jnp.zeros_like(squares)

    squares[...] += square


def total_kernel(near, same, cross, fold, dq_squares, mine, theirs, sums):
    total = near[...] + same[...].astype(jnp.float32) + cross[...].astype(jnp.float32)
    total = total + fold[...].astype(jnp.float32)
    total = total.astype(mine.dtype)
    half = mine.shape[1]
    mine[...] = total[:, :half]
    theirs[...] = total[:, half:]
    wide = total.astype(jnp.float32)
    square = jnp.sum((wide * wide).reshape(-1, 8, wide.shape[-1]), axis=0)
    square = jnp.sum(square, keepdims=True) + jnp.sum(dq_squares[...], keepdims=True)
    sums[...] = jnp.broadcast_to(square, sums.shape)


def call(kernel, groups, ins, outs, flops, exps, *args, grant=VMEM):
    return pl.pallas_call(
        kernel,
        grid_spec=pltpu.PrefetchScalarGridSpec(
            num_scalar_prefetch=1,
            grid=(groups,),
            in_specs=ins,
            out_specs=[spec for spec, _ in outs],
        ),
        out_shape=[shape for _, shape in outs],
        compiler_params=pltpu.CompilerParams(vmem_limit_bytes=grant),
        cost_estimate=pl.CostEstimate(
            flops=flops, bytes_accessed=4 * 1024 * 1024, transcendentals=exps
        ),
    )(*args)


def all_sum(x, axes):
    given = lax.all_to_all(x, axes, 0, 0, tiled=True)
    return jnp.sum(given, axis=0, keepdims=True)


def body(queries, keys, values, output_gradient_stored):
    q, k, v, g = queries[0], keys[0], values[0], output_gradient_stored[0]
    contexts, heads = lax.axis_size("ctx"), lax.axis_size("head")
    quarter = heads // 2
    ctx, head = lax.axis_index("ctx"), lax.axis_index("head")
    core = head % 2
    core_pairs = [(h, h ^ 1) for h in range(heads)]
    side_pairs = [(h, h ^ 2) for h in range(heads) if h & 2 == 0]
    side_back = [(target, source) for source, target in side_pairs]

    def flat(c, h):
        return c * heads + h

    chain = []
    for h in range(quarter):
        chain += [(flat(c, h), flat(c + 1, h)) for c in range(contexts - 1)]
        chain += [(flat(c, h + quarter), flat(c - 1, h + quarter)) for c in range(1, contexts)]
    slant = [(source, target ^ 2) for source, target in chain]
    last = contexts - 1
    fold_far = [(flat(last, h), flat(last, (h + quarter) ^ 2)) for h in range(quarter)]
    fold_near = [(flat(last, h), flat(last, h ^ 2)) for h in range(quarter, heads)]
    fold_near_back = [(flat(last, h), flat(last, h ^ 2)) for h in range(quarter)]
    fold_far_back = [(target, source) for source, target in fold_far]
    chain_back = [(target, source) for source, target in chain]
    slant_back = [(target, source) for source, target in slant] + fold_far_back
    both = ("ctx", "head")

    def swap_core(x):
        return lax.ppermute(x, "head", core_pairs)

    def cut(x, which):
        width = x.shape[1] // 2
        return lax.dynamic_slice_in_dim(x, which * width, width, axis=1)

    rows = q.shape[0]
    kv_theirs = swap_core(jnp.stack([cut(k, 1 - core), cut(v, 1 - core)]))
    own = jnp.concatenate([jnp.stack([cut(k, core), cut(v, core)]), kv_theirs], axis=1)
    fold_cross = lax.ppermute(own, both, fold_far)
    side = lax.ppermute(own, "head", side_pairs)
    same = lax.ppermute(own, both, chain)
    cross = lax.ppermute(own, both, slant)
    qg_theirs = jnp.concatenate([cut(q, 1 - core), cut(g, 1 - core)], axis=1)
    qg_theirs, own_late = lax.optimization_barrier((qg_theirs, own))
    qg_theirs = swap_core(qg_theirs)
    late_head, qg_theirs = lax.optimization_barrier((head, qg_theirs))
    place = jnp.stack(
        [late_head % 2, (late_head // 2) % 2, jnp.where((ctx > 0) | (late_head >= quarter), 1, 0)]
    ).astype(jnp.int32)

    groups = own.shape[2] // HEAD_SIZE
    wide = GROUP * HEAD_SIZE
    span = own.shape[1]
    mine_spec = pl.BlockSpec((rows, wide), lambda j, p: (0, p[0] * groups + j))
    q_spec = pl.BlockSpec((rows, wide), lambda j, p: (0, j))
    g_spec = pl.BlockSpec((rows, wide), lambda j, p: (0, groups + j))
    kv_spec = pl.BlockSpec((2, span, HEAD_SIZE), lambda j, p: (0, 0, j))
    k_spec = pl.BlockSpec((1, span, HEAD_SIZE), lambda j, p: (0, 0, j))
    stat_spec = pl.BlockSpec((1, 4 * GROUP, span), lambda j, p: (j, 0, 0))
    ds_spec = pl.BlockSpec((1, GROUP, 3 * span, span), lambda j, p: (j, 0, 0, 0))
    square_spec = pl.BlockSpec((8, HEAD_SIZE), lambda j, p: (0, 0))
    qg_specs = [mine_spec, q_spec, mine_spec, g_spec]
    stat = (stat_spec, jax.ShapeDtypeStruct((groups, 4 * GROUP, span), jnp.float32))
    grad = (kv_spec, jax.ShapeDtypeStruct(own.shape, q.dtype))
    part = (q_spec, jax.ShapeDtypeStruct((rows, groups * wide), q.dtype))
    unit = 2 * span * span * HEAD_SIZE * groups * GROUP
    exps = span * span * groups * GROUP
    rows_in = (place, q, qg_theirs, g, qg_theirs)

    (own_stats,) = call(
        own_kernel, groups, qg_specs + [kv_spec], [stat], 2 * unit, exps, *rows_in, own
    )
    fold_first, own_stats = lax.optimization_barrier((fold_cross, own_stats))
    fold_same = lax.ppermute(fold_first, both, fold_near)
    side_grad, same_grad, cross_grad, dscores, stats = call(
        remote_kernel,
        groups,
        qg_specs + [stat_spec] + [kv_spec] * 5,
        [grad] * 3
        + [(ds_spec, jax.ShapeDtypeStruct((groups, GROUP, 3 * span, span), q.dtype)), stat],
        12 * unit,
        3 * exps,
        *rows_in, own_stats, side, same, cross, fold_same, fold_cross,
    )
    fold_grad = lax.ppermute(same_grad, both, fold_far_back)
    from_side = lax.ppermute(side_grad, "head", side_back)
    next_same = lax.ppermute(same_grad, both, chain_back)
    next_cross = lax.ppermute(cross_grad, both, slant_back)
    dq_mine, dq_theirs, own_grad, dq_squares = call(
        rest_kernel,
        groups,
        qg_specs + [stat_spec, kv_spec] + [k_spec] * 5 + [ds_spec],
        [part, part, (kv_spec, jax.ShapeDtypeStruct(own.shape, jnp.float32))]
        + [(square_spec, jax.ShapeDtypeStruct((8, HEAD_SIZE), jnp.float32))],
        8 * unit,
        exps,
        *rows_in, stats, own, side, same, cross, fold_same, fold_cross, dscores, grant=60 * 1024 * 1024,
    )
    fold_grad, dq_squares = lax.optimization_barrier((fold_grad, dq_squares))
    from_fold = lax.ppermute(fold_grad, both, fold_near_back)
    dq_back = swap_core(dq_theirs)
    near = own_grad + from_side.astype(jnp.float32)
    dq_squares = jnp.sum(dq_squares, axis=0, keepdims=True)
    half_shape = jax.ShapeDtypeStruct((2, rows, own.shape[2]), q.dtype)
    total_mine, total_theirs, sums = pl.pallas_call(
        total_kernel,
        out_shape=[half_shape, half_shape, jax.ShapeDtypeStruct((heads, HEAD_SIZE), jnp.float32)],
        compiler_params=pltpu.CompilerParams(vmem_limit_bytes=24 * 1024 * 1024),
    )(near, next_same, next_cross, from_fold, dq_squares)

    def join(mine, theirs):
        low = jnp.where(core == 0, mine, theirs)
        high = jnp.where(core == 0, theirs, mine)
        return jnp.concatenate([low, high], axis=-1)

    grad_q = join(dq_mine, dq_back)
    sums = all_sum(sums, "head")
    grad_kv = join(total_mine, swap_core(total_theirs))
    norm_square = all_sum(jnp.broadcast_to(sums, (2 * contexts, HEAD_SIZE)), ("dp", "ctx"))[0, 0]
    return (grad_q[None], grad_kv[0][None], grad_kv[1][None], jnp.sqrt(norm_square))


def solution(mesh):
    spec = P("dp", ("ctx", "head"), None)
    return jax.shard_map(
        body,
        mesh=mesh,
        in_specs=(spec, spec, spec, spec),
        out_specs=(spec, spec, spec, P()),
        check_vma=False,
    )
```
